128 devices in a mesh: dp: 16 (over z, x), tensor: 8 (over y, core).
Axes of the slice: x: 4, y: 4, z: 4, core: 2. Of those that a mesh axis runs over, the one named last changes fastest.
Arguments:
- activations: bfloat16 [16384, 8192], P('dp'), may hold values from -6 to 6
- output_grads: bfloat16 [16384, 28672], P('dp', 'tensor'), may hold values from -0.046875 to 0.046875
- basis: bfloat16 [8192, 512], P('dp', 'tensor'), may hold values from -0.0625 to 0.0625
- first_in: float32 [512, 28672], P('dp', 'tensor'), may hold values from -6 to 6
- second_in: float32 [512, 28672], P('dp', 'tensor'), may hold values from 0.2 to 2
Outputs:
- projected_grad: float32 [512, 28672], P('dp', 'tensor')
- first_out: float32 [512, 28672], P('dp', 'tensor')
- second_out: float32 [512, 28672], P('dp', 'tensor')
- update: bfloat16 [8192, 28672], P('dp', 'tensor')
The draws below stay inside these ranges and needn't reach their ends.
All inputs are finite; a program needn't handle non-finite values.
Results may differ from the reference program's by a relative error of at most 0.0049.
Values may be sent and summed in bfloat16 or wider, within the bound.
A program may use at most 128 MiB of HBM per device.

```python
import math
import jax
import jax.numpy as jnp

D = 8192
FF = 28672
R = 512
STEP = 1000
TOKENS = 16384


def block_levels(rng, shape, shards, least, top_value):
    gain = 1.0
    for dim, blocks in shards:
        heights = jax.random.uniform(jax.random.fold_in(jax.random.fold_in(rng, 6), dim), (blocks,), jnp.float32, least / len(shards), top_value / len(shards))
        gain = gain * jnp.repeat(jnp.exp(heights), shape[dim] // blocks).reshape((-1,) + (1,) * (len(shape) - 1 - dim))
    return gain


def gaussian(own_key, shape, spread, most, pieces=(), kind=jnp.bfloat16):
    drawn = spread * jax.random.normal(own_key, shape, jnp.float32)
    if pieces:
        drawn = drawn * block_levels(own_key, shape, pieces, -0.22, 0.18)
    return jnp.clip(drawn, -most, most).astype(kind)


def setup_inputs(seed: int = 0) -> dict:
    splits = jax.random.split(jax.random.key(seed), 6)
    return {
        "activations": gaussian(splits[0], (TOKENS, D), 1.0, 6.0, ((0, 16),)),
        "output_grads": gaussian(splits[1], (TOKENS, FF), TOKENS ** -0.5, 0.046875, ((0, 16), (1, 8))),
        "basis": gaussian(splits[2], (D, R), D ** -0.5, 0.0625, ((0, 16), (1, 8))),
        "first_in": gaussian(splits[3], (R, FF), 1.0, 6.0, ((0, 16), (1, 8)), jnp.float32),
        "second_in": jnp.clip(jnp.exp(math.log(2.0) - 2.3025851 * jax.random.uniform(splits[4], (R, FF), jnp.float32) ** block_levels(splits[4], (R, FF), ((0, 16), (1, 8)), -0.2, 0.2)), 0.2, 2.0),
    }


beta_one = 0.9
beta_two = 0.999
adam_eps = 1e-08

def reference(activations, output_grads, basis, first_in, second_in):
    projected = jnp.dot(activations, basis, preferred_element_type=jnp.float32).astype(jnp.bfloat16)
    projected_grad = jnp.dot(projected.T, output_grads, preferred_element_type=jnp.float32)
    first_out = beta_one * first_in + (1.0 - beta_one) * projected_grad
    second_out = beta_two * second_in + (1.0 - beta_two) * projected_grad * projected_grad
    first_hat = first_out / (1.0 - beta_one ** STEP)
    second_hat = second_out / (1.0 - beta_two ** STEP)
    normalized = (first_hat / (jnp.sqrt(second_hat) + adam_eps)).astype(jnp.bfloat16)
    update = jnp.dot(basis, normalized, preferred_element_type=jnp.float32).astype(jnp.bfloat16)
    return (projected_grad, first_out, second_out, update)
```

```python
import functools

import jax
import jax.numpy as jnp
from jax import lax
from jax.experimental import pallas as pl
from jax.experimental.pallas import tpu as pltpu
from jax.sharding import PartitionSpec as P

STEP = 1000

beta_one = 0.9
beta_two = 0.999
adam_eps = 1e-08

MESH = pl.DeviceIdType.MESH
BF = jnp.bfloat16
F32 = jnp.float32

CHUNKS = 7
SIDE = 4
TO = (1, -1, 2)
FROM = (0, -1, 1, 2)

ORDER = [
    (0, 0), (0, 1), (0, 2), (0, 3), (0, 4), (0, 5), (1, 0), (1, 1), (0, 6), (1, 2),
    (1, 3), (1, 4), (1, 5), (2, 0), (2, 1), (1, 6), (2, 2), (2, 3), (2, 4), (2, 5),
    (3, 0), (3, 1), (2, 6), (3, 2), (3, 3), (3, 4), (3, 5), (4, 0), (4, 1), (3, 6),
    (4, 2), (4, 3), (4, 4), (4, 5), (5, 0), (5, 1), (4, 6), (5, 2), (5, 3), (5, 4),
    (5, 5), (6, 0), (6, 1), (5, 6), (6, 2), (6, 3), (6, 4), (6, 5), (6, 6),
]


def adam(grad, first, second):
    first_out = beta_one * first + (1.0 - beta_one) * grad
    second_out = beta_two * second + (1.0 - beta_two) * grad * grad
    return first_out, second_out


def step_of(first_out, second_out):
    first_hat = first_out / (1.0 - beta_one**STEP)
    second_hat = second_out / (1.0 - beta_two**STEP)
    return (first_hat / (jnp.sqrt(second_hat) + adam_eps)).astype(BF)


def exchange(
    acts, grads, basis, first, second,
    norm_out, rows_out, grad_out,
    act_v, grads_v, basis_v, first_v, second_v, packs, rows_packs, rows_v, acc, turned,
    part, send1, send2, send3, recv1, recv2, recv3, norm, grad_v,
    load_s, w1s, w1r, w2s, w2r, bs, br, ys, yr, s1, r1, s2, r2, s3, r3, s5, r5, s7, r7, s8, r8,
    out_s,
):
    dp, tensor = lax.axis_index("dp"), lax.axis_index("tensor")
    z, x, y, core = dp // SIDE, dp % SIDE, tensor // 2, tensor % 2
    width = grads_v.shape[2]
    half = width // 2

    def near(at, step):
        return lax.rem(at + step + SIDE, SIDE)

    def along(axis, step):
        if axis == "z":
            return (near(z, step) * SIDE + x, tensor)
        if axis == "x":
            return (z * SIDE + near(x, step), tensor)
        if axis == "y":
            return (dp, near(y, step) * 2 + core)
        return (dp, y * 2 + (1 - core))

    sent = []

    def send(src, dst, ssem, rsem, device):
        copy = pltpu.make_async_remote_copy(
            src_ref=src, dst_ref=dst, send_sem=ssem, recv_sem=rsem,
            device_id=device, device_id_type=MESH,
        )
        copy.start()
        sent.append(copy)
        return copy

    def got(ref, ssem, rsem, device):
        pltpu.make_async_remote_copy(
            src_ref=ref, dst_ref=ref, send_sem=ssem, recv_sem=rsem,
            device_id=device, device_id_type=MESH,
        ).wait_recv()

    def load(src, dst, n):
        copy = pltpu.make_async_copy(src, dst, load_s.at[n])
        copy.start()
        return copy

    order = [(0, 0), (0, 1), (0, 2), (1, 0), (2, 0), (0, 3), (3, 0)]
    order += [(a, b) for a in (1, 2) for b in (1, 2)]
    order += [(1, 3), (2, 3), (3, 1), (3, 2), (3, 3)]
    depth = act_v.shape[2]
    loaded_basis = load(basis, basis_v, 0)
    loaded_acts = []
    for n, (a, b) in enumerate(order):
        block = near(z, FROM[a]) * SIDE + near(x, FROM[b])
        columns = pl.ds(pl.multiple_of(block * depth, depth), depth)
        loaded_acts.append(load(acts.at[:, columns], act_v.at[n], 1 + n))
    loaded_grads = [
        load(grads.at[:, pl.ds(k * width, width)], grads_v.at[k], 17 + k) for k in range(CHUNKS)
    ]
    loaded_first = load(first, first_v, 17 + CHUNKS)
    loaded_second = load(second, second_v, 18 + CHUNKS)

    barrier = pltpu.get_barrier_semaphore()
    partners = [along(axis, step) for axis in "zxy" for step in TO] + [along("core", 1)]
    for device in partners:
        pl.semaphore_signal(barrier, inc=1, device_id=device, device_id_type=MESH)
    loaded_basis.wait()
    top = depth // 2
    pack = jnp.concatenate([basis_v[:top], basis_v[top:]], axis=1)
    packs[z, x] = pack
    rows_packs[tensor] = pack
    pl.semaphore_wait(barrier, len(partners))

    ends = (pl.ds(0, top // 2), pl.ds(top // 2, top // 2))

    def spot(path, m, i):
        a, b = (i, m) if path == 0 else (m, i)
        return packs.at[near(z, FROM[a]), near(x, FROM[b]), ends[path]]

    lead, trail = ("x", "z"), ("z", "x")
    for path in (0, 1):
        for i in range(3):
            send(spot(path, 0, 0), spot(path, 0, 0), w1s.at[path, i], w1r.at[path, i], along(lead[path], TO[i]))

    def onward(path, m):
        for i in range(3):
            send(spot(path, m, 0), spot(path, m, 0), w2s.at[path, m, i], w2r.at[path, m, i], along(trail[path], TO[i]))

    onward(0, 0)
    onward(1, 0)

    def spread(buffer, ssem, rsem):
        own = buffer.at[tensor]
        send(own, own, ssem.at[0], rsem.at[0], along("core", 1))
        for i in range(3):
            send(own, own, ssem.at[1 + i], rsem.at[1 + i], along("y", TO[i]))

    def forward(buffer, ssem, rsem):
        for i in range(3):
            block = buffer.at[near(y, FROM[1 + i]) * 2 + core]
            got(block, ssem.at[1 + i], rsem.at[1 + i], along("y", TO[i]))
            send(block, block, ssem.at[4 + i], rsem.at[4 + i], along("core", 1))

    def collected(buffer, ssem, rsem):
        for n in (0, 4, 5, 6):
            got(buffer.at[0], ssem.at[n], rsem.at[n], along("core", 1))

    spread(rows_packs, bs, br)

    def project(n):
        a, b = order[n]
        loaded_acts[n].wait()
        weights = packs[near(z, FROM[a]), near(x, FROM[b])]
        for side in (0, 1):
            term = jnp.dot(
                act_v[n, :, side * top : (side + 1) * top], weights, preferred_element_type=F32
            )
            acc[side] = term if n == 0 else acc[side] + term

    def arrived(n):
        a, b = order[n]
        for path, m, i in ((0, b, a), (1, a, b)):
            if i > 0:
                got(spot(path, m, i), w2s.at[path, m, i - 1], w2r.at[path, m, i - 1], along(trail[path], 1))

    def first_hop(i):
        for path in (0, 1):
            got(spot(path, i, 0), w1s.at[path, i - 1], w1r.at[path, i - 1], along(lead[path], 1))
            onward(path, i)

    project(0)
    for i in (1, 2, 3):
        first_hop(i)
    for n in range(1, len(order)):
        arrived(n)
        project(n)

    rank = turned.shape[1]
    total = acc[0] + pltpu.roll(acc[1], rank, 1)
    turned[tensor] = total.T[:rank].astype(BF)
    spread(turned, ys, yr)
    forward(rows_packs, bs, br)
    forward(turned, ys, yr)
    collected(rows_packs, bs, br)
    for n in range(SIDE):
        even, odd = rows_packs[2 * n], rows_packs[2 * n + 1]
        lanes = pl.ds(n * 2 * rank, 2 * rank)
        rows_v[:top, lanes] = jnp.concatenate([even[:, :rank], odd[:, :rank]], axis=1)
        rows_v[top:, lanes] = jnp.concatenate([even[:, rank:], odd[:, rank:]], axis=1)
    stores = []

    def store(src, dst, n):
        copy = pltpu.make_async_copy(src, dst, out_s.at[n])
        copy.start()
        stores.append(copy)

    store(rows_v, rows_out, CHUNKS)
    loaded_first.wait()
    loaded_second.wait()
    collected(turned, ys, yr)

    axes = (("z", "x"), ("x", "z"))
    places = ((z, x), (x, z))

    def lanes_of(path):
        return pl.ds(path * half, half)

    def slab(ref, path, place, low=0, count=SIDE):
        if path == 0:
            return ref.at[place, pl.ds(low, count)]
        return ref.at[pl.ds(low, count), place]

    def partial(path, k, place, low=0, count=SIDE):
        if path == 0:
            return part[k, place, low : low + count, :, lanes_of(path)]
        return part[k, low : low + count, place, :, lanes_of(path)]

    def columns_of(path, k):
        return pl.ds(k * width + path * half, half)

    def stage0(k):
        loaded_grads[k].wait()
        lhs = turned[...].reshape(2 * SIDE * rank, turned.shape[2])
        product = jnp.dot(lhs, grads_v[k], preferred_element_type=F32)
        part[k] = product.reshape(part.shape[1:])
        for path in (0, 1):
            far = near(places[path][0], 2)
            for d in (0, 1):
                send1[path, k, d] = partial(path, k, far, 2 * d, 2).astype(BF)
                send(send1.at[path, k, d], recv1.at[path, k, d], s1.at[path, k, d], r1.at[path, k, d], along(axes[path][0], TO[d]))

    def stage1(k):
        for path in (0, 1):
            for d in (0, 1):
                got(recv1.at[path, k, d], s1.at[path, k, d], r1.at[path, k, d], along(axes[path][0], TO[d]))
                to = near(places[path][0], TO[d])
                joined = partial(path, k, to, 2 * d, 2) + recv1[path, k, d].astype(F32)
                send2[path, k, d, 2 * d : 2 * d + 2] = joined.astype(BF)
                other = 2 - 2 * d
                send2[path, k, d, other : other + 2] = partial(path, k, to, other, 2).astype(BF)
                send(send2.at[path, k, d], recv2.at[path, k, d], s2.at[path, k, d], r2.at[path, k, d], along(axes[path][0], TO[d]))

    def stage2(k):
        for path in (0, 1):
            here, there = places[path]
            for d in (0, 1):
                got(recv2.at[path, k, d], s2.at[path, k, d], r2.at[path, k, d], along(axes[path][0], TO[d]))
            total = partial(path, k, here) + recv2[path, k, 0].astype(F32) + recv2[path, k, 1].astype(F32)
            if path == 0:
                part[k, here, :, :, lanes_of(path)] = total
            else:
                part[k, :, here, :, lanes_of(path)] = total
            for i in range(3):
                to = near(there, TO[i])
                row = (here, to) if path == 0 else (to, here)
                send3[path, k, i] = part[k, row[0], row[1], :, lanes_of(path)].astype(BF)
                send(send3.at[path, k, i], recv3.at[path, k, i], s3.at[path, k, i], r3.at[path, k, i], along(axes[path][1], TO[i]))

    def stage3(k):
        for path in (0, 1):
            for i in range(3):
                got(recv3.at[path, k, i], s3.at[path, k, i], r3.at[path, k, i], along(axes[path][1], TO[i]))
            total = part[k, z, x, :, lanes_of(path)]
            for i in range(3):
                total = total + recv3[path, k, i].astype(F32)
            columns = columns_of(path, k)
            grad_v[:, columns] = total
            norm[z, x, :, columns] = step_of(*adam(total, first_v[:, columns], second_v[:, columns]))
            own = norm.at[z, x, :, columns]
            for i in range(3):
                send(own, own, s5.at[path, k, i], r5.at[path, k, i], along(axes[path][1], TO[i]))

    def stage4(k):
        for path in (0, 1):
            columns = columns_of(path, k)
            for i in range(3):
                got(norm.at[0, 0, :, columns], s5.at[path, k, i], r5.at[path, k, i], along(axes[path][1], TO[i]))
            block = slab(norm, path, places[path][0]).at[:, :, columns]
            for d in (0, 1):
                send(block, block, s7.at[path, k, d], r7.at[path, k, d], along(axes[path][0], TO[d]))

    def stage5(k):
        for path in (0, 1):
            columns = columns_of(path, k)
            for d in (0, 1):
                place = near(places[path][0], FROM[1 + d])
                got(slab(norm, path, place).at[:, :, columns], s7.at[path, k, d], r7.at[path, k, d], along(axes[path][0], TO[d]))
                block = slab(norm, path, place, 2 * d, 2).at[:, :, columns]
                send(block, block, s8.at[path, k, d], r8.at[path, k, d], along(axes[path][0], TO[d]))

    def stage6(k):
        for path in (0, 1):
            columns = columns_of(path, k)
            for d in (0, 1):
                place = near(places[path][0], 2)
                got(slab(norm, path, place, 2 * d, 2).at[:, :, columns], s8.at[path, k, d], r8.at[path, k, d], along(axes[path][0], TO[d]))
        columns = pl.ds(k * width, width)
        store(norm.at[:, :, :, columns], norm_out.at[:, :, :, columns], k)

    stages = (stage0, stage1, stage2, stage3, stage4, stage5, stage6)
    summed = 0
    for stage, k in ORDER:
        stages[stage](k)
        if stage == 3:
            summed += 1
            if summed == CHUNKS:
                store(grad_v, grad_out, CHUNKS + 1)
    for copy in sent:
        copy.wait_send()
    for copy in stores:
        copy.wait()


def finish(norm, rows, grad, first, second, grad_out, first_out, second_out, update):
    grad_out[...] = grad[...]
    first_out[...], second_out[...] = adam(grad[...], first[...], second[...])
    update[...] = jnp.dot(rows[...], norm[...], preferred_element_type=F32).astype(BF)


def local(acts, grads, basis, first, second):
    tokens, width = acts.shape
    rows, rank = basis.shape
    own, units = first.shape
    wide = units // CHUNKS
    half = wide // 2
    pairs = (2, CHUNKS)
    vmem, dma = pltpu.VMEM, pltpu.SemaphoreType.DMA
    whole = pl.BlockSpec(memory_space=pl.ANY)
    norm, rows_all, grad = pl.pallas_call(
        exchange,
        out_shape=(
            jax.ShapeDtypeStruct((SIDE, SIDE, own, units), BF),
            jax.ShapeDtypeStruct((rows, 8 * rank), BF),
            jax.ShapeDtypeStruct((own, units), F32),
        ),
        in_specs=[whole] * 5,
        out_specs=[whole] * 3,
        scratch_shapes=[
            vmem((16, tokens, rows), BF),
            vmem((CHUNKS, tokens, wide), BF),
            vmem((rows, rank), BF),
            vmem((own, units), F32),
            vmem((own, units), F32),
            vmem((SIDE, SIDE, rows // 2, 2 * rank), BF),
            vmem((8, rows // 2, 2 * rank), BF),
            vmem((rows, 8 * rank), BF),
            vmem((2, tokens, 2 * rank), F32),
            vmem((8, rank, tokens), BF),
            vmem((CHUNKS, SIDE, SIDE, own, wide), F32),
            vmem((*pairs, 2, 2, own, half), BF),
            vmem((*pairs, 2, SIDE, own, half), BF),
            vmem((*pairs, 3, own, half), BF),
            vmem((*pairs, 2, 2, own, half), BF),
            vmem((*pairs, 2, SIDE, own, half), BF),
            vmem((*pairs, 3, own, half), BF),
            vmem((SIDE, SIDE, own, units), BF),
            vmem((own, units), F32),
            dma((19 + CHUNKS,)),
            dma((2, 3)), dma((2, 3)), dma((2, 4, 3)), dma((2, 4, 3)),
            dma((7,)), dma((7,)), dma((7,)), dma((7,)),
            dma((*pairs, 2)), dma((*pairs, 2)), dma((*pairs, 2)), dma((*pairs, 2)),
            dma((*pairs, 3)), dma((*pairs, 3)), dma((*pairs, 3)), dma((*pairs, 3)),
            dma((*pairs, 2)), dma((*pairs, 2)), dma((*pairs, 2)), dma((*pairs, 2)),
            dma((CHUNKS + 2,)),
        ],
        compiler_params=pltpu.CompilerParams(
            collective_id=0, has_side_effects=True, vmem_limit_bytes=60 << 20
        ),
        name="exchange",
    )(acts, grads, basis, first, second)
    columns = lambda n: pl.BlockSpec((n, wide), lambda k: (0, k))
    return pl.pallas_call(
        finish,
        grid=(CHUNKS,),
        out_shape=(
            jax.ShapeDtypeStruct((own, units), F32),
            jax.ShapeDtypeStruct((own, units), F32),
            jax.ShapeDtypeStruct((own, units), F32),
            jax.ShapeDtypeStruct((rows, units), BF),
        ),
        in_specs=[
            columns(16 * own),
            pl.BlockSpec((rows, 8 * rank), lambda k: (0, 0)),
            columns(own),
            columns(own),
            columns(own),
        ],
        out_specs=(columns(own), columns(own), columns(own), columns(rows)),
        compiler_params=pltpu.CompilerParams(vmem_limit_bytes=32 << 20),
        name="finish",
    )(norm.reshape(16 * own, units), rows_all, grad, first, second)


def solution(mesh):
    both = P("dp", "tensor")
    return jax.shard_map(
        local,
        mesh=mesh,
        in_specs=(P("dp", None), both, both, both, both),
        out_specs=(both, both, both, both),
        check_vma=False,
    )
```

```python
import functools

import jax
import jax.numpy as jnp
from jax import lax
from jax.experimental import pallas as pl
from jax.experimental.pallas import tpu as pltpu
from jax.sharding import PartitionSpec as P

STEP = 1000

beta_one = 0.9
beta_two = 0.999
adam_eps = 1e-08

MESH = pl.DeviceIdType.MESH
BF = jnp.bfloat16
F32 = jnp.float32

SIDE = 4
TO = (1, -1, 2)
FROM = (0, -1, 1, 2)

PIECE = 512
UNITS = [
    (0, 0, 512), (0, 512, 1024), (0, 1536, 1024), (0, 2560, 1024),
    (1, 0, 1024), (1, 1024, 1024), (1, 2048, 1024), (1, 3072, 512),
]
ORDER = [
    (0, 0), (0, 1), (7, 0), (0, 2), (1, 0), (0, 3), (1, 1), (8, 0),
    (0, 4), (1, 2), (2, 0), (0, 5), (1, 3), (2, 1), (0, 6), (1, 4), (2, 2), (0, 7), (3, 0),
    (1, 5), (2, 3), (3, 1), (1, 6), (2, 4), (3, 2), (1, 7), (2, 5), (3, 3), (4, 0),
    (2, 6), (3, 4), (4, 1), (2, 7), (3, 5), (4, 2), (3, 6), (5, 0), (4, 3), (3, 7), (5, 1),
    (4, 4), (5, 2), (4, 5), (5, 3), (4, 6), (5, 4), (4, 7), (5, 5), (6, 0), (6, 1), (6, 2),
    (5, 6), (5, 7), (6, 3), (6, 4), (6, 5), (6, 6), (6, 7),
]


def adam(grad, first, second):
    first_out = beta_one * first + (1.0 - beta_one) * grad
    second_out = beta_two * second + (1.0 - beta_two) * grad * grad
    return first_out, second_out


def step_of(first_out, second_out):
    first_hat = first_out / (1.0 - beta_one**STEP)
    second_hat = second_out / (1.0 - beta_two**STEP)
    return (first_hat / (jnp.sqrt(second_hat) + adam_eps)).astype(BF)


def exchange(
    acts, grads, basis, first, second,
    norm, rows_v, grad_v, first_o, second_o,
    act_v, grads_v, basis_v, first_v, second_v, packs, rows_packs, acc, turned,
    part, send1, send2, send3, recv1, recv2, recv3,
    load_s, send_s, hop_r, block_r, tensor_r, unit_r,
):
    dp, tensor = lax.axis_index("dp"), lax.axis_index("tensor")
    z, x, y, core = dp // SIDE, dp % SIDE, tensor // 2, tensor % 2
    depth = act_v.shape[2]
    own = norm.shape[2] // 2

    def near(at, step):
        return lax.rem(at + step + SIDE, SIDE)

    def along(axis, step):
        if axis == "z":
            return (near(z, step) * SIDE + x, tensor)
        if axis == "x":
            return (z * SIDE + near(x, step), tensor)
        if axis == "y":
            return (dp, near(y, step) * 2 + core)
        return (dp, y * 2 + (1 - core))

    def send(ref, to, kind, rsem, device):
        pltpu.make_async_remote_copy(
            src_ref=ref, dst_ref=to, send_sem=send_s.at[kind], recv_sem=rsem,
            device_id=device, device_id_type=MESH,
        ).start()

    def got(like, rsem):
        pltpu.make_async_remote_copy(
            src_ref=like, dst_ref=like, send_sem=send_s.at[0], recv_sem=rsem,
            device_id=along("core", 1), device_id_type=MESH,
        ).wait_recv()

    def all_sent(like, kind):
        pltpu.make_async_remote_copy(
            src_ref=like, dst_ref=like, send_sem=send_s.at[kind], recv_sem=unit_r.at[0, 0],
            device_id=along("core", 1), device_id_type=MESH,
        ).wait_send()

    def load(src, dst, n):
        copy = pltpu.make_async_copy(src, dst, load_s.at[n])
        copy.start()
        return copy

    order = [(0, 0), (0, 1), (0, 2), (1, 0), (2, 0), (0, 3), (3, 0)]
    order += [(a, b) for a in (1, 2) for b in (1, 2)]
    order += [(1, 3), (2, 3), (3, 1), (3, 2), (3, 3)]
    loaded_basis = load(basis, basis_v, 0)
    for n, (a, b) in enumerate(order):
        block = near(z, FROM[a]) * SIDE + near(x, FROM[b])
        columns = pl.ds(pl.multiple_of(block * depth, depth), depth)
        load(acts.at[:, columns], act_v.at[n], 1 + n // 2)

    barrier = pltpu.get_barrier_semaphore()
    partners = [along(axis, step) for axis in "zxy" for step in TO] + [along("core", 1)]
    for device in partners:
        pl.semaphore_signal(barrier, inc=1, device_id=device, device_id_type=MESH)
    loaded_basis.wait()
    rows_packs[tensor] = basis_v[...]
    for h in (0, 1):
        packs[h, z, x, :own] = basis_v[h * own : (h + 1) * own]
        packs[h, z, x, own:] = basis_v[(h + 2) * own : (h + 3) * own]
    pl.semaphore_wait(barrier, len(partners))

    lead, trail = ("x", "z"), ("z", "x")

    def spot(h, path, m, i):
        a, b = (i, m) if path == 0 else (m, i)
        return packs.at[h, near(z, FROM[a]), near(x, FROM[b]), pl.ds(path * own, own)]

    def onward(h, path, m):
        block = spot(h, path, m, 0)
        for i in range(3):
            n = order.index((i + 1, m) if path == 0 else (m, i + 1))
            send(block, block, 0, block_r.at[h, n], along(trail[path], TO[i]))

    def outset(h):
        for path in (0, 1):
            block = spot(h, path, 0, 0)
            for i in range(3):
                send(block, block, 0, hop_r.at[h, i], along(lead[path], TO[i]))
        for path in (0, 1):
            onward(h, path, 0)

    def first_hop(h, m):
        got(packs.at[h, 0, 0], hop_r.at[h, m - 1])
        for path in (0, 1):
            onward(h, path, m)

    def project(h, n):
        a, b = order[n]
        if n > 0:
            halves = 2 if a > 0 and b > 0 else 1
            got(packs.at[h, 0, 0, pl.ds(0, halves * own)], block_r.at[h, n])
        if h == 0 and n % 2 == 0:
            two = act_v.at[pl.ds(n, 2)]
            pltpu.make_async_copy(two, two, load_s.at[1 + n // 2]).wait()
        block = packs[h, near(z, FROM[a]), near(x, FROM[b])]
        term = lax.dot_general(
            block, act_v[n], (((1,), (1,)), ((), ())), preferred_element_type=F32
        )
        acc[h] = term if n == 0 else acc[h] + term

    def spread(buffer, rsem):
        block = buffer.at[tensor]
        send(block, block, 1, rsem.at[3], along("core", 1))
        for i in range(3):
            send(block, block, 1, rsem.at[i], along("y", TO[i]))

    def forward(buffer, rsem):
        for i in range(3):
            block = buffer.at[near(y, FROM[1 + i]) * 2 + core]
            got(block, rsem.at[i])
            send(block, block, 1, rsem.at[3], along("core", 1))

    def collected(buffer, rsem):
        got(buffer.at[pl.ds(0, SIDE)], rsem.at[3])

    def rounded(h):
        turned[h, tensor] = acc[h].astype(BF)
        spread(turned.at[h], tensor_r.at[h])

    outset(0)
    spread(rows_packs, tensor_r.at[2])
    project(0, 0)
    for m in (1, 2, 3):
        first_hop(0, m)
    outset(1)
    for n in range(1, 7):
        project(0, n)
    for m in (1, 2, 3):
        first_hop(1, m)
    for n in range(7, 16):
        project(0, n)
    rounded(0)
    loaded_grads = []
    for u in range(len(UNITS) // 2):
        columns = pl.ds(*UNITS[u][1:])
        loaded_grads.append(load(grads.at[:, columns], grads_v.at[:, columns], 9 + u))
    loaded_moments = [load(first, first_v, 13), load(second, second_v, 14)]
    for n in range(0, 10):
        project(1, n)
    forward(turned.at[0], tensor_r.at[0])
    for n in range(10, 16):
        project(1, n)
    rounded(1)
    forward(rows_packs, tensor_r.at[2])
    collected(turned.at[0], tensor_r.at[0])

    axes = (("z", "x"), ("x", "z"))
    places = ((z, x), (x, z))

    def lanes(path, u, base):
        _, low, count = UNITS[u]
        return pl.ds(low + path * count // 2 if base else low // 2, count // 2)

    def slab(ref, path, place, low=0, count=SIDE):
        if path == 0:
            return ref.at[place, pl.ds(low, count)]
        return ref.at[pl.ds(low, count), place]

    def rows(u):
        return pl.ds(UNITS[u][0] * own, own)

    def partial(path, u, place, low=0, count=SIDE):
        ref = slab(part.at[UNITS[u][0]], path, place, low, count)
        return ref[:, :, lanes(path, u, True)]

    def message(buffer, path, u, n):
        return buffer.at[path, UNITS[u][0], n].at[..., lanes(path, u, False)]

    def take(like, u, kind):
        got(like.at[:, UNITS[u][0]].at[..., lanes(0, u, False)], unit_r.at[kind, u])

    def stage0(u):
        h, low, count = UNITS[u]
        if h == 0:
            loaded_grads[u].wait()
        lhs = turned[h].reshape(16 * own, turned.shape[3])
        product = jnp.dot(lhs, grads_v[:, low : low + count], preferred_element_type=F32)
        part[h, :, :, :, low : low + count] = product.reshape(SIDE, SIDE, own, count)
        for path in (0, 1):
            far = near(places[path][0], 2)
            for d in (0, 1):
                out = message(send1, path, u, d)
                out[...] = partial(path, u, far, 2 * d, 2).astype(BF)
                to = along(axes[path][0], TO[d])
                send(out, message(recv1, path, u, d), 2, unit_r.at[0, u], to)

    def stage1(u):
        take(recv1, u, 0)
        for path in (0, 1):
            for d in (0, 1):
                arrived = message(recv1, path, u, d)
                to = near(places[path][0], TO[d])
                out = message(send2, path, u, d)
                joined = partial(path, u, to, 2 * d, 2) + arrived[...].astype(F32)
                out[2 * d : 2 * d + 2] = joined.astype(BF)
                other = 2 - 2 * d
                out[other : other + 2] = partial(path, u, to, other, 2).astype(BF)
                to = along(axes[path][0], TO[d])
                send(out, message(recv2, path, u, d), 3, unit_r.at[1, u], to)

    def stage2(u):
        take(recv2, u, 1)
        for path in (0, 1):
            here, there = places[path]
            total = partial(path, u, here)
            for d in (0, 1):
                total = total + message(recv2, path, u, d)[...].astype(F32)
            ref = slab(part.at[UNITS[u][0]], path, here)
            columns = lanes(path, u, True)
            ref[:, :, columns] = total
            for i in range(3):
                out = message(send3, path, u, i)
                out[...] = ref[near(there, TO[i]), :, columns].astype(BF)
                to = along(axes[path][1], TO[i])
                send(out, message(recv3, path, u, i), 4, unit_r.at[2, u], to)

    def stage3(u):
        if u == 0:
            for copy in loaded_moments:
                copy.wait()
        take(recv3, u, 2)
        for path in (0, 1):
            columns = lanes(path, u, True)
            total = part[UNITS[u][0], z, x, :, columns]
            for i in range(3):
                total = total + message(recv3, path, u, i)[...].astype(F32)
            at = rows(u), columns
            moments = adam(total, first_v[at], second_v[at])
            grad_v[at] = total
            first_o[at], second_o[at] = moments
            norm[z, x, rows(u), columns] = step_of(*moments)
            block = norm.at[z, x, rows(u), columns]
            for i in range(3):
                send(block, block, 5, unit_r.at[3, u], along(axes[path][1], TO[i]))

    def stage4(u):
        take(recv3, u, 3)
        for path in (0, 1):
            block = slab(norm, path, places[path][0]).at[:, rows(u), lanes(path, u, True)]
            for d in (0, 1):
                send(block, block, 6, unit_r.at[4, u], along(axes[path][0], TO[d]))

    def stage5(u):
        take(recv2, u, 4)
        for path in (0, 1):
            for d in (0, 1):
                place = near(places[path][0], FROM[1 + d])
                block = slab(norm, path, place, 2 * d, 2).at[:, rows(u), lanes(path, u, True)]
                send(block, block, 7, unit_r.at[5, u], along(axes[path][0], TO[d]))

    def stage6(u):
        take(recv1, u, 5)

    def stage7(_):
        forward(turned.at[1], tensor_r.at[1])

    def stage8(_):
        collected(turned.at[1], tensor_r.at[1])
        collected(rows_packs, tensor_r.at[2])
        whole = rows_packs[...].reshape(rows_v.shape[1], rows_v.shape[0])
        rows_v[...] = whole.astype(F32).T.astype(BF)

    stages = (stage0, stage1, stage2, stage3, stage4, stage5, stage6, stage7, stage8)
    for stage, u in ORDER:
        stages[stage](u)
    all_sent(act_v.at[0, pl.ds(0, 2 * 30 * own)], 0)
    all_sent(act_v.at[pl.ds(0, 3), pl.ds(0, 7 * rows_packs.shape[1])], 1)
    for kind, like in ((2, send1), (3, send2), (4, send3), (5, send3), (6, send2), (7, send1)):
        all_sent(like, kind)


def finish(norm, rows, grad, first, second, grad_out, first_out, second_out, update, tiles, sems):
    copies = []

    def store(src, dst):
        copies.append(pltpu.make_async_copy(src, dst, sems.at[len(copies)]))
        copies[-1].start()

    wide = tiles.shape[2]
    for k in range(tiles.shape[0]):
        columns = pl.ds(k * wide, wide)
        tiles[k] = jnp.dot(rows[...], norm[:, columns], preferred_element_type=F32).astype(BF)
        store(tiles.at[k], update.at[:, columns])
        if k == 0:
            for src, dst in ((grad, grad_out), (first, first_out), (second, second_out)):
                store(src, dst)
    for copy in copies:
        copy.wait()


def local(acts, grads, basis, first, second):
    tokens = acts.shape[0]
    rank, rows = basis.shape
    own, units = first.shape
    pieces = units // PIECE
    vmem, dma = pltpu.VMEM, pltpu.SemaphoreType.DMA
    whole = pl.BlockSpec(memory_space=pl.ANY)
    norm, *rest = pl.pallas_call(
        exchange,
        out_shape=(
            vmem((SIDE, SIDE, own, units), BF),
            vmem((rows, 8 * rank), BF),
            vmem((own, units), F32),
            vmem((own, units), F32),
            vmem((own, units), F32),
        ),
        in_specs=[whole] * 5,
        out_specs=[pl.BlockSpec(memory_space=vmem)] * 5,
        scratch_shapes=[
            vmem((16, tokens, rows), BF),
            vmem((tokens, units), BF),
            vmem((rank, rows), BF),
            vmem((own, units), F32),
            vmem((own, units), F32),
            vmem((2, SIDE, SIDE, own, rows), BF),
            vmem((8, rank, rows), BF),
            vmem((2, own, tokens), F32),
            vmem((2, 8, own, tokens), BF),
            vmem((2, SIDE, SIDE, own // 2, units), F32),
            vmem((2, 2, 2, 2, own // 2, units // 2), BF),
            vmem((2, 2, 2, SIDE, own // 2, units // 2), BF),
            vmem((2, 2, 3, own // 2, units // 2), BF),
            vmem((2, 2, 2, 2, own // 2, units // 2), BF),
            vmem((2, 2, 2, SIDE, own // 2, units // 2), BF),
            vmem((2, 2, 3, own // 2, units // 2), BF),
            dma((15,)), dma((8,)), dma((2, 3)), dma((2, 16)), dma((3, 4)), dma((6, len(UNITS))),
        ],
        compiler_params=pltpu.CompilerParams(
            collective_id=0, has_side_effects=True, vmem_limit_bytes=50 << 20
        ),
        name="exchange",
    )(acts, grads, basis, first, second)
    return pl.pallas_call(
        finish,
        out_shape=(
            jax.ShapeDtypeStruct((own, units), F32),
            jax.ShapeDtypeStruct((own, units), F32),
            jax.ShapeDtypeStruct((own, units), F32),
            jax.ShapeDtypeStruct((rows, units), BF),
        ),
        in_specs=[pl.BlockSpec(memory_space=vmem)] * 5,
        out_specs=[pl.BlockSpec(memory_space=pltpu.HBM)] * 4,
        scratch_shapes=[vmem((pieces, rows, PIECE), BF), dma((pieces + 3,))],
        compiler_params=pltpu.CompilerParams(vmem_limit_bytes=16 << 20),
        name="finish",
    )(norm.reshape(16 * own, units), *rest)


def solution(mesh):
    both = P("dp", "tensor")

    def step(acts, grads, basis, first, second):
        return local(acts, grads, basis.T, first, second)

    return jax.shard_map(
        step,
        mesh=mesh,
        in_specs=(P("dp", None), both, both, both, both),
        out_specs=(both, both, both, both),
        check_vma=False,
    )
```

```python
import functools

import jax
import jax.numpy as jnp
from jax import lax
from jax.experimental import pallas as pl
from jax.experimental.pallas import tpu as pltpu
from jax.sharding import PartitionSpec as P

STEP = 1000

beta_one = 0.9
beta_two = 0.999
adam_eps = 1e-08

MESH = pl.DeviceIdType.MESH
BF = jnp.bfloat16
F32 = jnp.float32

SIDE = 4
TO = (1, -1, 2)
FROM = (0, -1, 1, 2)

PIECE = 512
UNITS = [
    (0, 0, 512), (0, 512, 1024), (0, 1536, 1024), (0, 2560, 1024),
    (1, 0, 1024), (1, 1024, 1024), (1, 2048, 1024), (1, 3072, 512),
]
ORDER = [
    (0, 0), (0, 1), (0, 2), (0, 3), (7, 0), (1, 0), (1, 1), (1, 2), (8, 0), (0, 4),
    (0, 5), (0, 6), (0, 7), (1, 3), (2, 0), (2, 1), (1, 4), (1, 5), (1, 6), (1, 7),
    (2, 2), (2, 3), (3, 0), (2, 4), (3, 1), (2, 5), (2, 6), (2, 7), (3, 2), (3, 3),
    (3, 4), (4, 0), (3, 5), (3, 6), (3, 7), (4, 1), (4, 2), (4, 3), (4, 4), (5, 0),
    (4, 5), (4, 6), (4, 7), (5, 1), (5, 2), (5, 3), (5, 4), (6, 0), (5, 5), (5, 6),
    (5, 7), (6, 1), (6, 2), (6, 3), (6, 4), (6, 5), (6, 6), (6, 7),
]


def adam(grad, first, second):
    first_out = beta_one * first + (1.0 - beta_one) * grad
    second_out = beta_two * second + (1.0 - beta_two) * grad * grad
    return first_out, second_out


def step_of(first_out, second_out):
    first_hat = first_out / (1.0 - beta_one**STEP)
    second_hat = second_out / (1.0 - beta_two**STEP)
    return (first_hat / (jnp.sqrt(second_hat) + adam_eps)).astype(BF)


def exchange(
    acts, grads, basis, first, second,
    norm, rows_v, grad_v, first_o, second_o,
    act_v, grads_v, basis_v, first_v, second_v, packs, rows_packs, acc, turned,
    part, send1, send2, send3, recv1, recv2, recv3,
    load_s, send_s, hop_r, block_r, tensor_r, unit_r,
):
    dp, tensor = lax.axis_index("dp"), lax.axis_index("tensor")
    z, x, y, core = dp // SIDE, dp % SIDE, tensor // 2, tensor % 2
    depth = act_v.shape[2]
    own = norm.shape[2] // 2

    def near(at, step):
        return lax.rem(at + step + SIDE, SIDE)

    def along(axis, step):
        if axis == "z":
            return (near(z, step) * SIDE + x, tensor)
        if axis == "x":
            return (z * SIDE + near(x, step), tensor)
        if axis == "y":
            return (dp, near(y, step) * 2 + core)
        return (dp, y * 2 + (1 - core))

    def send(ref, to, kind, rsem, device):
        pltpu.make_async_remote_copy(
            src_ref=ref, dst_ref=to, send_sem=send_s.at[kind], recv_sem=rsem,
            device_id=device, device_id_type=MESH,
        ).start()

    def got(like, rsem):
        pltpu.make_async_remote_copy(
            src_ref=like, dst_ref=like, send_sem=send_s.at[0], recv_sem=rsem,
            device_id=along("core", 1), device_id_type=MESH,
        ).wait_recv()

    def all_sent(like, kind):
        pltpu.make_async_remote_copy(
            src_ref=like, dst_ref=like, send_sem=send_s.at[kind], recv_sem=unit_r.at[0, 0],
            device_id=along("core", 1), device_id_type=MESH,
        ).wait_send()

    def load(src, dst, n):
        copy = pltpu.make_async_copy(src, dst, load_s.at[n])
        copy.start()
        return copy

    order = [(0, 0), (0, 1), (0, 2), (1, 0), (2, 0), (0, 3), (3, 0)]
    order += [(a, b) for a in (1, 2) for b in (1, 2)]
    order += [(1, 3), (2, 3), (3, 1), (3, 2), (3, 3)]
    loaded_basis = load(basis, basis_v, 0)
    for n, (a, b) in enumerate(order):
        block = near(z, FROM[a]) * SIDE + near(x, FROM[b])
        columns = pl.ds(pl.multiple_of(block * depth, depth), depth)
        load(acts.at[:, columns], act_v.at[n], 1 + n // 2)

    barrier = pltpu.get_barrier_semaphore()
    partners = [along(axis, step) for axis in "zxy" for step in TO] + [along("core", 1)]
    for device in partners:
        pl.semaphore_signal(barrier, inc=1, device_id=device, device_id_type=MESH)
    loaded_basis.wait()
    rows_packs[tensor] = basis_v[...]
    for h in (0, 1):
        packs[h, z, x, :own] = basis_v[h * own : (h + 1) * own]
        packs[h, z, x, own:] = basis_v[(h + 2) * own : (h + 3) * own]
    pl.semaphore_wait(barrier, len(partners))

    lead, trail = ("x", "z"), ("z", "x")

    def spot(h, path, m, i):
        a, b = (i, m) if path == 0 else (m, i)
        return packs.at[h, near(z, FROM[a]), near(x, FROM[b]), pl.ds(path * own, own)]

    def onward(h, path, m):
        block = spot(h, path, m, 0)
        for i in range(3):
            n = order.index((i + 1, m) if path == 0 else (m, i + 1))
            send(block, block, 0, block_r.at[h, n], along(trail[path], TO[i]))

    def outset(h):
        for path in (0, 1):
            block = spot(h, path, 0, 0)
            for i in range(3):
                send(block, block, 0, hop_r.at[h, i], along(lead[path], TO[i]))
        for path in (0, 1):
            onward(h, path, 0)

    def first_hop(h, m):
        got(packs.at[h, 0, 0], hop_r.at[h, m - 1])
        for path in (0, 1):
            onward(h, path, m)

    def project(h, n):
        a, b = order[n]
        if n > 0:
            halves = 2 if a > 0 and b > 0 else 1
            got(packs.at[h, 0, 0, pl.ds(0, halves * own)], block_r.at[h, n])
        if h == 0 and n % 2 == 0:
            two = act_v.at[pl.ds(n, 2)]
            pltpu.make_async_copy(two, two, load_s.at[1 + n // 2]).wait()
        block = packs[h, near(z, FROM[a]), near(x, FROM[b])]
        term = lax.dot_general(
            block, act_v[n], (((1,), (1,)), ((), ())), preferred_element_type=F32
        )
        acc[h] = term if n == 0 else acc[h] + term

    def spread(buffer, rsem):
        block = buffer.at[tensor]
        for i in (2, 0, 1):
            send(block, block, 1, rsem.at[i], along("y", TO[i]))
        send(block, block, 1, rsem.at[3], along("core", 1))

    def forward(buffer, rsem):
        for i in range(3):
            block = buffer.at[near(y, FROM[1 + i]) * 2 + core]
            got(block, rsem.at[i])
            send(block, block, 1, rsem.at[3], along("core", 1))

    def collected(buffer, rsem):
        got(buffer.at[pl.ds(0, SIDE)], rsem.at[3])

    def rounded(h):
        turned[h, tensor] = acc[h].astype(BF)
        spread(turned.at[h], tensor_r.at[h])

    outset(0)
    spread(rows_packs, tensor_r.at[2])
    project(0, 0)
    for m in (1, 2, 3):
        first_hop(0, m)
    outset(1)
    for n in range(1, 11):
        project(0, n)
    first_hop(1, 1)
    first_hop(1, 2)
    for n in range(11, 16):
        project(0, n)
    rounded(0)
    first_hop(1, 3)
    loaded_grads = []
    for u in range(sum(unit[0] == 0 for unit in UNITS)):
        columns = pl.ds(*UNITS[u][1:])
        loaded_grads.append(load(grads.at[:, columns], grads_v.at[:, columns], 11 + u))
    loaded_moments = [load(first, first_v, 9), load(second, second_v, 10)]
    for n in range(0, 10):
        project(1, n)
    forward(turned.at[0], tensor_r.at[0])
    for n in range(10, 16):
        project(1, n)
    rounded(1)
    forward(rows_packs, tensor_r.at[2])
    collected(turned.at[0], tensor_r.at[0])

    axes = (("z", "x"), ("x", "z"))
    places = ((z, x), (x, z))

    def lanes(path, u, base):
        _, low, count = UNITS[u]
        return pl.ds(low + path * count // 2 if base else low // 2, count // 2)

    def slab(ref, path, place, low=0, count=SIDE):
        if path == 0:
            return ref.at[place, pl.ds(low, count)]
        return ref.at[pl.ds(low, count), place]

    def rows(u):
        return pl.ds(UNITS[u][0] * own, own)

    def partial(path, u, place, low=0, count=SIDE):
        ref = slab(part.at[UNITS[u][0]], path, place, low, count)
        return ref[:, :, lanes(path, u, True)]

    def message(buffer, path, u, n):
        return buffer.at[path, UNITS[u][0], n].at[..., lanes(path, u, False)]

    def take(like, u, kind):
        got(like.at[:, UNITS[u][0]].at[..., lanes(0, u, False)], unit_r.at[kind, u])

    def stage0(u):
        h, low, count = UNITS[u]
        if h == 0:
            loaded_grads[u].wait()
        lhs = turned[h].reshape(16 * own, turned.shape[3])
        product = jnp.dot(lhs, grads_v[:, low : low + count], preferred_element_type=F32)
        part[h, :, :, :, low : low + count] = product.reshape(SIDE, SIDE, own, count)
        for path in (0, 1):
            far = near(places[path][0], 2)
            for d in (0, 1):
                out = message(send1, path, u, d)
                out[...] = partial(path, u, far, 2 * d, 2).astype(BF)
                to = along(axes[path][0], TO[d])
                send(out, message(recv1, path, u, d), 2, unit_r.at[0, u], to)

    def stage1(u):
        take(recv1, u, 0)
        for path in (0, 1):
            for d in (0, 1):
                arrived = message(recv1, path, u, d)
                to = near(places[path][0], TO[d])
                out = message(send2, path, u, d)
                joined = partial(path, u, to, 2 * d, 2) + arrived[...].astype(F32)
                out[2 * d : 2 * d + 2] = joined.astype(BF)
                other = 2 - 2 * d
                out[other : other + 2] = partial(path, u, to, other, 2).astype(BF)
                to = along(axes[path][0], TO[d])
                send(out, message(recv2, path, u, d), 3, unit_r.at[1, u], to)

    def stage2(u):
        take(recv2, u, 1)
        for path in (0, 1):
            here, there = places[path]
            total = partial(path, u, here)
            for d in (0, 1):
                total = total + message(recv2, path, u, d)[...].astype(F32)
            ref = slab(part.at[UNITS[u][0]], path, here)
            columns = lanes(path, u, True)
            ref[:, :, columns] = total
            for i in range(3):
                out = message(send3, path, u, i)
                out[...] = ref[near(there, TO[i]), :, columns].astype(BF)
                to = along(axes[path][1], TO[i])
                send(out, message(recv3, path, u, i), 4, unit_r.at[2, u], to)

    def stage3(u):
        if u == 0:
            for copy in loaded_moments:
                copy.wait()
        take(recv3, u, 2)
        for path in (0, 1):
            columns = lanes(path, u, True)
            total = part[UNITS[u][0], z, x, :, columns]
            for i in range(3):
                total = total + message(recv3, path, u, i)[...].astype(F32)
            at = rows(u), columns
            moments = adam(total, first_v[at], second_v[at])
            grad_v[at] = total
            first_o[at], second_o[at] = moments
            norm[z, x, rows(u), columns] = step_of(*moments)
            block = norm.at[z, x, rows(u), columns]
            for i in range(3):
                send(block, block, 5, unit_r.at[3, u], along(axes[path][1], TO[i]))

    def stage4(u):
        take(recv3, u, 3)
        for path in (0, 1):
            block = slab(norm, path, places[path][0]).at[:, rows(u), lanes(path, u, True)]
            for d in (0, 1):
                send(block, block, 6, unit_r.at[4, u], along(axes[path][0], TO[d]))

    def stage5(u):
        take(recv2, u, 4)
        for path in (0, 1):
            for d in (0, 1):
                place = near(places[path][0], FROM[1 + d])
                block = slab(norm, path, place, 2 * d, 2).at[:, rows(u), lanes(path, u, True)]
                send(block, block, 7, unit_r.at[5, u], along(axes[path][0], TO[d]))

    def stage6(u):
        take(recv1, u, 5)

    def stage7(_):
        forward(turned.at[1], tensor_r.at[1])

    def stage8(_):
        collected(turned.at[1], tensor_r.at[1])
        collected(rows_packs, tensor_r.at[2])
        whole = rows_packs[...].reshape(rows_v.shape[1], rows_v.shape[0])
        rows_v[...] = whole.astype(F32).T.astype(BF)

    stages = (stage0, stage1, stage2, stage3, stage4, stage5, stage6, stage7, stage8)
    for stage, u in ORDER:
        stages[stage](u)
    all_sent(act_v.at[0, pl.ds(0, 2 * 30 * own)], 0)
    all_sent(act_v.at[pl.ds(0, 3), pl.ds(0, 7 * rows_packs.shape[1])], 1)
    for kind, like in ((2, send1), (3, send2), (4, send3), (5, send3), (6, send2), (7, send1)):
        all_sent(like, kind)


def finish(norm, rows, grad, first, second, grad_out, first_out, second_out, update, tiles, sems):
    copies = []

    def store(src, dst):
        copies.append(pltpu.make_async_copy(src, dst, sems.at[len(copies)]))
        copies[-1].start()

    wide = tiles.shape[2]
    for src, dst in ((grad, grad_out), (first, first_out), (second, second_out)):
        store(src, dst)
    for k in range(tiles.shape[0]):
        columns = pl.ds(k * wide, wide)
        tiles[k] = jnp.dot(rows[...], norm[:, columns], preferred_element_type=F32).astype(BF)
        store(tiles.at[k], update.at[:, columns])
    for copy in copies:
        copy.wait()


def local(acts, grads, basis, first, second):
    tokens = acts.shape[0]
    rank, rows = basis.shape
    own, units = first.shape
    pieces = units // PIECE
    vmem, dma = pltpu.VMEM, pltpu.SemaphoreType.DMA
    whole = pl.BlockSpec(memory_space=pl.ANY)
    norm, *rest = pl.pallas_call(
        exchange,
        out_shape=(
            vmem((SIDE, SIDE, own, units), BF),
            vmem((rows, 8 * rank), BF),
            vmem((own, units), F32),
            vmem((own, units), F32),
            vmem((own, units), F32),
        ),
        in_specs=[whole] * 5,
        out_specs=[pl.BlockSpec(memory_space=vmem)] * 5,
        scratch_shapes=[
            vmem((16, tokens, rows), BF),
            vmem((tokens, units), BF),
            vmem((rank, rows), BF),
            vmem((own, units), F32),
            vmem((own, units), F32),
            vmem((2, SIDE, SIDE, own, rows), BF),
            vmem((8, rank, rows), BF),
            vmem((2, own, tokens), F32),
            vmem((2, 8, own, tokens), BF),
            vmem((2, SIDE, SIDE, own // 2, units), F32),
            vmem((2, 2, 2, 2, own // 2, units // 2), BF),
            vmem((2, 2, 2, SIDE, own // 2, units // 2), BF),
            vmem((2, 2, 3, own // 2, units // 2), BF),
            vmem((2, 2, 2, 2, own // 2, units // 2), BF),
            vmem((2, 2, 2, SIDE, own // 2, units // 2), BF),
            vmem((2, 2, 3, own // 2, units // 2), BF),
            dma((11 + len(UNITS),)), dma((8,)), dma((2, 3)), dma((2, 16)), dma((3, 4)), dma((6, len(UNITS))),
        ],
        compiler_params=pltpu.CompilerParams(
            collective_id=0, has_side_effects=True, vmem_limit_bytes=50 << 20
        ),
        name="exchange",
    )(acts, grads, basis, first, second)
    return pl.pallas_call(
        finish,
        out_shape=(
            jax.ShapeDtypeStruct((own, units), F32),
            jax.ShapeDtypeStruct((own, units), F32),
            jax.ShapeDtypeStruct((own, units), F32),
            jax.ShapeDtypeStruct((rows, units), BF),
        ),
        in_specs=[pl.BlockSpec(memory_space=vmem)] * 5,
        out_specs=[pl.BlockSpec(memory_space=pltpu.HBM)] * 4,
        scratch_shapes=[vmem((pieces, rows, PIECE), BF), dma((pieces + 3,))],
        compiler_params=pltpu.CompilerParams(vmem_limit_bytes=16 << 20),
        name="finish",
    )(norm.reshape(16 * own, units), *rest)


def solution(mesh):
    both = P("dp", "tensor")

    def step(acts, grads, basis, first, second):
        return local(acts, grads, basis.T, first, second)

    return jax.shard_map(
        step,
        mesh=mesh,
        in_specs=(P("dp", None), both, both, both, both),
        out_specs=(both, both, both, both),
        check_vma=False,
    )
```

```python
import functools

import jax
import jax.numpy as jnp
from jax import lax
from jax.experimental import pallas as pl
from jax.experimental.pallas import tpu as pltpu
from jax.sharding import PartitionSpec as P

STEP = 1000

beta_one = 0.9
beta_two = 0.999
adam_eps = 1e-08

MESH = pl.DeviceIdType.MESH
BF = jnp.bfloat16
F32 = jnp.float32

SIDE = 4
TO = (1, -1, 2)
FROM = (0, -1, 1, 2)

PIECE = 512
UNITS = [
    (0, 0, 512), (0, 512, 1024), (0, 1536, 1024), (0, 2560, 1024),
    (1, 0, 1024), (1, 1024, 1024), (1, 2048, 1024), (1, 3072, 512),
]
ORDER = [
    (0, 0), (0, 1), (0, 2), (0, 3), (7, 0), (1, 0), (1, 1), (1, 2), (8, 0), (0, 4),
    (0, 5), (0, 6), (0, 7), (1, 3), (2, 0), (2, 1), (1, 4), (1, 5), (1, 6), (1, 7),
    (2, 2), (2, 3), (3, 0), (2, 4), (3, 1), (2, 5), (2, 6), (2, 7), (3, 2), (3, 3),
    (3, 4), (4, 0), (3, 5), (3, 6), (3, 7), (4, 1), (4, 2), (4, 3), (4, 4), (5, 0),
    (4, 5), (4, 6), (4, 7), (5, 1), (5, 2), (5, 3), (5, 4), (6, 0), (5, 5), (5, 6),
    (5, 7), (6, 1), (6, 2), (6, 3), (6, 4), (6, 5), (6, 6), (6, 7),
]


def adam(grad, first, second):
    first_out = beta_one * first + (1.0 - beta_one) * grad
    second_out = beta_two * second + (1.0 - beta_two) * grad * grad
    return first_out, second_out


def step_of(first_out, second_out):
    first_hat = first_out / (1.0 - beta_one**STEP)
    second_hat = second_out / (1.0 - beta_two**STEP)
    return (first_hat / (jnp.sqrt(second_hat) + adam_eps)).astype(BF)


def exchange(
    acts, grads, basis, first, second,
    norm, rows_v, grad_v, first_o, second_o,
    act_v, grads_v, basis_v, first_v, second_v, packs, rows_packs, acc, turned,
    part, send1, send2, send3, recv1, recv2, recv3,
    load_s, send_s, hop_r, block_r, tensor_r, unit_r,
):
    dp, tensor = lax.axis_index("dp"), lax.axis_index("tensor")
    z, x, y, core = dp // SIDE, dp % SIDE, tensor // 2, tensor % 2
    depth = act_v.shape[2]
    own = norm.shape[2] // 2

    def near(at, step):
        return lax.rem(at + step + SIDE, SIDE)

    def along(axis, step):
        if axis == "z":
            return (near(z, step) * SIDE + x, tensor)
        if axis == "x":
            return (z * SIDE + near(x, step), tensor)
        if axis == "y":
            return (dp, near(y, step) * 2 + core)
        return (dp, y * 2 + (1 - core))

    def send(ref, to, kind, rsem, device):
        pltpu.make_async_remote_copy(
            src_ref=ref, dst_ref=to, send_sem=send_s.at[kind], recv_sem=rsem,
            device_id=device, device_id_type=MESH,
        ).start()

    def got(like, rsem):
        pltpu.make_async_remote_copy(
            src_ref=like, dst_ref=like, send_sem=send_s.at[0], recv_sem=rsem,
            device_id=along("core", 1), device_id_type=MESH,
        ).wait_recv()

    def all_sent(like, kind):
        pltpu.make_async_remote_copy(
            src_ref=like, dst_ref=like, send_sem=send_s.at[kind], recv_sem=unit_r.at[0, 0],
            device_id=along("core", 1), device_id_type=MESH,
        ).wait_send()

    def load(src, dst, n):
        copy = pltpu.make_async_copy(src, dst, load_s.at[n])
        copy.start()
        return copy

    order = [(0, 0), (0, 1), (0, 2), (1, 0), (2, 0), (0, 3), (3, 0)]
    order += [(a, b) for a in (1, 2) for b in (1, 2)]
    order += [(1, 3), (2, 3), (3, 1), (3, 2), (3, 3)]
    loaded_basis = load(basis, basis_v, 0)

    barrier = pltpu.get_barrier_semaphore()
    partners = [along(axis, step) for axis in "zxy" for step in TO] + [along("core", 1)]
    for device in partners:
        pl.semaphore_signal(barrier, inc=1, device_id=device, device_id_type=MESH)

    def load_acts(low, high):
        for n in range(low, high):
            a, b = order[n]
            block = near(z, FROM[a]) * SIDE + near(x, FROM[b])
            columns = pl.ds(pl.multiple_of(block * depth, depth), depth)
            load(acts.at[:, columns], act_v.at[n], 1 + n // 2)

    load_acts(0, 6)
    loaded_basis.wait()
    rows_packs[tensor] = basis_v[...]
    for h in (0, 1):
        packs[h, z, x, :own] = basis_v[h * own : (h + 1) * own]
        packs[h, z, x, own:] = basis_v[(h + 2) * own : (h + 3) * own]
    pl.semaphore_wait(barrier, len(partners))

    lead, trail = ("x", "z"), ("z", "x")

    def spot(h, path, m, i):
        a, b = (i, m) if path == 0 else (m, i)
        return packs.at[h, near(z, FROM[a]), near(x, FROM[b]), pl.ds(path * own, own)]

    def onward(h, path, m):
        block = spot(h, path, m, 0)
        for i in range(3):
            n = order.index((i + 1, m) if path == 0 else (m, i + 1))
            send(block, block, 0, block_r.at[h, n], along(trail[path], TO[i]))

    def outset(h):
        for path in (0, 1):
            block = spot(h, path, 0, 0)
            for i in range(3):
                send(block, block, 0, hop_r.at[h, i], along(lead[path], TO[i]))
        for path in (0, 1):
            onward(h, path, 0)

    def first_hop(h, m):
        got(packs.at[h, 0, 0], hop_r.at[h, m - 1])
        for path in (0, 1):
            onward(h, path, m)

    def project(h, n):
        a, b = order[n]
        if n > 0:
            halves = 2 if a > 0 and b > 0 else 1
            got(packs.at[h, 0, 0, pl.ds(0, halves * own)], block_r.at[h, n])
        if h == 0 and n % 2 == 0:
            two = act_v.at[pl.ds(n, 2)]
            pltpu.make_async_copy(two, two, load_s.at[1 + n // 2]).wait()
        block = packs[h, near(z, FROM[a]), near(x, FROM[b])]
        term = lax.dot_general(
            block, act_v[n], (((1,), (1,)), ((), ())), preferred_element_type=F32
        )
        acc[h] = term if n == 0 else acc[h] + term

    def spread(buffer, rsem):
        block = buffer.at[tensor]
        for i in (2, 0, 1):
            send(block, block, 1, rsem.at[i], along("y", TO[i]))
        send(block, block, 1, rsem.at[3], along("core", 1))

    def forward(buffer, rsem):
        for i in range(3):
            block = buffer.at[near(y, FROM[1 + i]) * 2 + core]
            got(block, rsem.at[i])
            send(block, block, 1, rsem.at[3], along("core", 1))

    def collected(buffer, rsem):
        got(buffer.at[pl.ds(0, SIDE)], rsem.at[3])

    def rounded(h):
        turned[h, tensor] = acc[h].astype(BF)
        spread(turned.at[h], tensor_r.at[h])

    outset(0)
    load_acts(6, 16)
    spread(rows_packs, tensor_r.at[2])
    project(0, 0)
    for m in (1, 2, 3):
        first_hop(0, m)
    outset(1)
    for n in range(1, 11):
        project(0, n)
    first_hop(1, 1)
    first_hop(1, 2)
    for n in range(11, 16):
        project(0, n)
    rounded(0)
    first_hop(1, 3)
    loaded_grads = []
    for u in range(sum(unit[0] == 0 for unit in UNITS)):
        columns = pl.ds(*UNITS[u][1:])
        loaded_grads.append(load(grads.at[:, columns], grads_v.at[:, columns], 11 + u))
    loaded_moments = [load(first, first_v, 9), load(second, second_v, 10)]
    for n in range(0, 10):
        project(1, n)
    forward(turned.at[0], tensor_r.at[0])
    for n in range(10, 16):
        project(1, n)
    rounded(1)
    forward(rows_packs, tensor_r.at[2])
    collected(turned.at[0], tensor_r.at[0])

    axes = (("z", "x"), ("x", "z"))
    places = ((z, x), (x, z))

    def lanes(path, u, base):
        _, low, count = UNITS[u]
        return pl.ds(low + path * count // 2 if base else low // 2, count // 2)

    def slab(ref, path, place, low=0, count=SIDE):
        if path == 0:
            return ref.at[place, pl.ds(low, count)]
        return ref.at[pl.ds(low, count), place]

    def rows(u):
        return pl.ds(UNITS[u][0] * own, own)

    def partial(path, u, place, low=0, count=SIDE):
        ref = slab(part.at[UNITS[u][0]], path, place, low, count)
        return ref[:, :, lanes(path, u, True)]

    def message(buffer, path, u, n):
        return buffer.at[path, UNITS[u][0], n].at[..., lanes(path, u, False)]

    def take(like, u, kind):
        got(like.at[:, UNITS[u][0]].at[..., lanes(0, u, False)], unit_r.at[kind, u])

    def stage0(u):
        h, low, count = UNITS[u]
        if h == 0:
            loaded_grads[u].wait()
        lhs = turned[h].reshape(16 * own, turned.shape[3])
        product = jnp.dot(lhs, grads_v[:, low : low + count], preferred_element_type=F32)
        part[h, :, :, :, low : low + count] = product.reshape(SIDE, SIDE, own, count)
        for path in (0, 1):
            far = near(places[path][0], 2)
            for d in (0, 1):
                out = message(send1, path, u, d)
                out[...] = partial(path, u, far, 2 * d, 2).astype(BF)
                to = along(axes[path][0], TO[d])
                send(out, message(recv1, path, u, d), 2, unit_r.at[0, u], to)

    def stage1(u):
        take(recv1, u, 0)
        for path in (0, 1):
            for d in (0, 1):
                arrived = message(recv1, path, u, d)
                to = near(places[path][0], TO[d])
                out = message(send2, path, u, d)
                joined = partial(path, u, to, 2 * d, 2) + arrived[...].astype(F32)
                out[2 * d : 2 * d + 2] = joined.astype(BF)
                other = 2 - 2 * d
                out[other : other + 2] = partial(path, u, to, other, 2).astype(BF)
                to = along(axes[path][0], TO[d])
                send(out, message(recv2, path, u, d), 3, unit_r.at[1, u], to)

    def stage2(u):
        take(recv2, u, 1)
        for path in (0, 1):
            here, there = places[path]
            total = partial(path, u, here)
            for d in (0, 1):
                total = total + message(recv2, path, u, d)[...].astype(F32)
            ref = slab(part.at[UNITS[u][0]], path, here)
            columns = lanes(path, u, True)
            ref[:, :, columns] = total
            for i in range(3):
                out = message(send3, path, u, i)
                out[...] = ref[near(there, TO[i]), :, columns].astype(BF)
                to = along(axes[path][1], TO[i])
                send(out, message(recv3, path, u, i), 4, unit_r.at[2, u], to)

    def stage3(u):
        if u == 0:
            for copy in loaded_moments:
                copy.wait()
        take(recv3, u, 2)
        for path in (0, 1):
            columns = lanes(path, u, True)
            total = part[UNITS[u][0], z, x, :, columns]
            for i in range(3):
                total = total + message(recv3, path, u, i)[...].astype(F32)
            at = rows(u), columns
            moments = adam(total, first_v[at], second_v[at])
            grad_v[at] = total
            first_o[at], second_o[at] = moments
            norm[z, x, rows(u), columns] = step_of(*moments)
            block = norm.at[z, x, rows(u), columns]
            for i in range(3):
                send(block, block, 5, unit_r.at[3, u], along(axes[path][1], TO[i]))

    def stage4(u):
        take(recv3, u, 3)
        for path in (0, 1):
            block = slab(norm, path, places[path][0]).at[:, rows(u), lanes(path, u, True)]
            for d in (0, 1):
                send(block, block, 6, unit_r.at[4, u], along(axes[path][0], TO[d]))

    def stage5(u):
        take(recv2, u, 4)
        for path in (0, 1):
            for d in (0, 1):
                place = near(places[path][0], FROM[1 + d])
                block = slab(norm, path, place, 2 * d, 2).at[:, rows(u), lanes(path, u, True)]
                send(block, block, 7, unit_r.at[5, u], along(axes[path][0], TO[d]))

    def stage6(u):
        take(recv1, u, 5)

    def stage7(_):
        forward(turned.at[1], tensor_r.at[1])

    def stage8(_):
        collected(turned.at[1], tensor_r.at[1])
        collected(rows_packs, tensor_r.at[2])
        whole = rows_packs[...].reshape(rows_v.shape[1], rows_v.shape[0])
        rows_v[...] = whole.astype(F32).T.astype(BF)

    stages = (stage0, stage1, stage2, stage3, stage4, stage5, stage6, stage7, stage8)
    for stage, u in ORDER:
        stages[stage](u)
    all_sent(act_v.at[0, pl.ds(0, 2 * 30 * own)], 0)
    all_sent(act_v.at[pl.ds(0, 3), pl.ds(0, 7 * rows_packs.shape[1])], 1)
    for kind, like in ((2, send1), (3, send2), (4, send3), (5, send3), (6, send2), (7, send1)):
        all_sent(like, kind)


def finish(norm, rows, grad, first, second, grad_out, first_out, second_out, update, tiles, sems):
    copies = []

    def store(src, dst):
        copies.append(pltpu.make_async_copy(src, dst, sems.at[len(copies)]))
        copies[-1].start()

    wide = tiles.shape[2]
    for src, dst in ((grad, grad_out), (first, first_out), (second, second_out)):
        store(src, dst)
    for k in range(tiles.shape[0]):
        columns = pl.ds(k * wide, wide)
        tiles[k] = jnp.dot(rows[...], norm[:, columns], preferred_element_type=F32).astype(BF)
        store(tiles.at[k], update.at[:, columns])
    for copy in copies:
        copy.wait()


def local(acts, grads, basis, first, second):
    tokens = acts.shape[0]
    rank, rows = basis.shape
    own, units = first.shape
    pieces = units // PIECE
    vmem, dma = pltpu.VMEM, pltpu.SemaphoreType.DMA
    whole = pl.BlockSpec(memory_space=pl.ANY)
    norm, *rest = pl.pallas_call(
        exchange,
        out_shape=(
            vmem((SIDE, SIDE, own, units), BF),
            vmem((rows, 8 * rank), BF),
            vmem((own, units), F32),
            vmem((own, units), F32),
            vmem((own, units), F32),
        ),
        in_specs=[whole] * 5,
        out_specs=[pl.BlockSpec(memory_space=vmem)] * 5,
        scratch_shapes=[
            vmem((16, tokens, rows), BF),
            vmem((tokens, units), BF),
            vmem((rank, rows), BF),
            vmem((own, units), F32),
            vmem((own, units), F32),
            vmem((2, SIDE, SIDE, own, rows), BF),
            vmem((8, rank, rows), BF),
            vmem((2, own, tokens), F32),
            vmem((2, 8, own, tokens), BF),
            vmem((2, SIDE, SIDE, own // 2, units), F32),
            vmem((2, 2, 2, 2, own // 2, units // 2), BF),
            vmem((2, 2, 2, SIDE, own // 2, units // 2), BF),
            vmem((2, 2, 3, own // 2, units // 2), BF),
            vmem((2, 2, 2, 2, own // 2, units // 2), BF),
            vmem((2, 2, 2, SIDE, own // 2, units // 2), BF),
            vmem((2, 2, 3, own // 2, units // 2), BF),
            dma((11 + len(UNITS),)), dma((8,)), dma((2, 3)), dma((2, 16)), dma((3, 4)), dma((6, len(UNITS))),
        ],
        compiler_params=pltpu.CompilerParams(
            collective_id=0, has_side_effects=True, vmem_limit_bytes=50 << 20
        ),
        name="exchange",
    )(acts, grads, basis, first, second)
    return pl.pallas_call(
        finish,
        out_shape=(
            jax.ShapeDtypeStruct((own, units), F32),
            jax.ShapeDtypeStruct((own, units), F32),
            jax.ShapeDtypeStruct((own, units), F32),
            jax.ShapeDtypeStruct((rows, units), BF),
        ),
        in_specs=[pl.BlockSpec(memory_space=vmem)] * 5,
        out_specs=[pl.BlockSpec(memory_space=pltpu.HBM)] * 4,
        scratch_shapes=[vmem((pieces, rows, PIECE), BF), dma((pieces + 3,))],
        compiler_params=pltpu.CompilerParams(vmem_limit_bytes=16 << 20),
        name="finish",
    )(norm.reshape(16 * own, units), *rest)


def solution(mesh):
    both = P("dp", "tensor")

    def step(acts, grads, basis, first, second):
        return local(acts, grads, basis.T, first, second)

    return jax.shard_map(
        step,
        mesh=mesh,
        in_specs=(P("dp", None), both, both, both, both),
        out_specs=(both, both, both, both),
        check_vma=False,
    )
```
